256 devices in a mesh: shift: 2 (over core), row: 32 (over z, x), col: 4 (over y).
Axes of the slice: x: 4, y: 4, z: 8, core: 2. Of those that a mesh axis runs over, the one named last changes fastest.
Arguments:
- root_inverse: float32 [8192, 4096], P(('shift', 'row'), 'col'), parts along dimension 0, may hold values from -12 to 12, as said below
- pattern: int32 [16], P('shift'), parts along dimension 0, may hold values from 0 to 15, as said below
- child_rows: float32 [2048, 4096], P(('shift', 'row'), 'col'), parts along dimension 0, may hold values from -1.5 to 1.5
- child_inverse: float32 [8192, 4096], P(('shift', 'row'), 'col'), parts along dimension 0, may hold values from -12 to 12
Outputs:
- coupling: float32 [2048, 4096], P(('shift', 'row'), 'col'), parts along dimension 0
- selected_inverse: float32 [8192, 4096], P(('shift', 'row'), 'col'), parts along dimension 0
The draws below stay inside these ranges and needn't reach their ends.
There are 2 independent parts, one for each index of `shift`. The reference program is written for one: setup_inputs(seed, part) draws one part's arguments, and reference() takes and returns one part's arrays. A program takes and returns all parts, laid end to end along the dimension named above; each array names one. Nothing has to cross between parts.
Inputs may be any that keep to these rules, and one draw needn't show every extreme that they name: `pattern`: 8 distinct block indices in increasing order, all among the root's first W // B // 2 blocks (indices 0 to W // B // 2 - 1, root rows 0 to W/2 - 1), the last being block W // B // 2 - 1. `root_inverse`: a symmetric matrix.
All inputs are finite; a program needn't handle non-finite values.
Results may differ from the reference program's by a relative error of at most 0.00011.
Values sent between devices are 32-bit elements; how exact they have to be, the bound alone decides.
No kernel may reach another device: no remote copies, remote signals or barrier semaphores. Data moves between devices by JAX's collectives and lax.ppermute only.
A program may use at most 64 MiB of HBM per device.

```python
import math
import jax
import jax.numpy as jnp
from jax import lax

W = 4096
WK = 4096
B = 128
NI = 8
M = 1024


def draw_root_inverse(key, part):
    key = jax.random.fold_in(key, 11)
    first, second = jax.random.split(key, 2)
    noise = jax.random.uniform(first, (W, W), jnp.float32, -1.0, 1.0)
    symmetric = (noise + noise.T) * (1.7 / math.sqrt(W))
    diagonal_vals = jax.random.uniform(second, (W,), jnp.float32, -1.6, 1.6)
    matrix = symmetric + jnp.diag(diagonal_vals)
    return matrix


def draw_pattern(key, part):
    key = jax.random.fold_in(key, 5)
    count = W // B // 2 - 1
    scores = jax.random.randint(key, (count,), 0, 1 << 20, dtype=jnp.int32) * count + jnp.arange(count, dtype=jnp.int32)
    chosen = jnp.argsort(scores, stable=True)[:NI - 1].astype(jnp.int32)
    last_block = jnp.full((1,), count, jnp.int32)
    return jnp.concatenate([jnp.sort(chosen), last_block]).astype(jnp.int32)


def levels(own_key, shape, pieces, low, top_value):
    loudness, own = 1.0, jax.random.fold_in(own_key, 6)
    for dim, shards_of in pieces:
        draws = jnp.exp(jax.random.uniform(jax.random.fold_in(own, dim), (shards_of,), jnp.float32, low / len(pieces), top_value / len(pieces)))
        loudness = loudness * jnp.repeat(draws, shape[dim] // shards_of).reshape([-1 if axis == dim else 1 for axis in range(len(shape))])
    return loudness


def bell_draw(rng, extent, deviation, reach, pieces=(), held_as=jnp.bfloat16):
    entries = jax.random.normal(rng, extent, jnp.float32) * deviation
    if len(pieces) > 0:
        entries = levels(rng, extent, pieces, -0.22, 0.18) * entries
    return jnp.clip(entries, min=-reach, max=reach).astype(held_as)


def setup_inputs(seed: int = 0, part: int = 0) -> dict:
    keys = jax.random.split(jax.random.key(seed), 5)
    own_keys = jax.random.split(jax.random.fold_in(keys[4], part), 5)
    root_inverse = draw_root_inverse(jax.random.fold_in(jax.random.fold_in(keys[4], part), 71), part)
    pattern = draw_pattern(jax.random.fold_in(jax.random.fold_in(keys[4], part), 71), part)
    child_rows = bell_draw(own_keys[2], (M, WK), 0.25, 1.5, ((0, 32), (1, 4)), jnp.float32)
    child_inverse = bell_draw(own_keys[3], (WK, WK), 2.0, 12.0, ((0, 32), (1, 4)), jnp.float32)
    return {"root_inverse": root_inverse, "pattern": pattern, "child_rows": child_rows, "child_inverse": child_inverse}


def reference(root_inverse, pattern, child_rows, child_inverse):
    within = jnp.arange(B, dtype=jnp.int32)
    root_index = (pattern[:, None] * B + within[None, :]).reshape(-1).astype(jnp.int32)
    picked = jnp.take(jnp.take(root_inverse, root_index, axis=0), root_index, axis=1)
    coupling = -jnp.dot(picked, child_rows, precision=lax.Precision.HIGHEST, preferred_element_type=jnp.float32)
    product = lax.dot_general(child_rows, coupling, (((0,), (0,)), ((), ())), precision=lax.Precision.HIGHEST, preferred_element_type=jnp.float32)
    return coupling, child_inverse - product
```

```python
import jax
import jax.numpy as jnp
from jax import lax
from jax.sharding import Mesh, PartitionSpec as P

B = 128
NZ, NX, NY = 8, 4, 4
HIGH = lax.Precision.HIGH


def shift_perm(n, d):
    return [(i, (i + d) % n) for i in range(n)]


def zxy(z, x, y):
    return (z * NX + x) * NY + y


def shards(root_inverse, pattern, child_rows, child_inverse):
    z = lax.axis_index("z")
    x = lax.axis_index("x")
    y = lax.axis_index("col")
    f32 = jnp.float32

    parts = [child_rows] + [
        lax.ppermute(child_rows, "x", shift_perm(NX, d)) for d in (1, 2, 3)
    ]
    block = jnp.zeros((NX, 32, 1024), f32)
    for d in range(NX):
        block = lax.dynamic_update_slice(
            block, parts[d][None], (lax.rem(x + NX - d, NX), 0, 0)
        )
    gathered = lax.all_gather(block.reshape(128, 1024), "z", axis=0, tiled=True)

    e = lax.rem(z, 2)
    perm = [
        (zxy(a, b, c), zxy(2 * c + a // 4, b, a % 4))
        for a in range(NZ) for b in range(NX) for c in range(NY)
    ]
    turned = lax.ppermute(child_rows, ("z", "x", "col"), perm).reshape(32, 2, 512)
    mine = lax.dynamic_slice_in_dim(turned, e, 1, axis=1).reshape(32, 512)
    other = lax.dynamic_slice_in_dim(turned, 1 - e, 1, axis=1).reshape(32, 512)
    other = lax.ppermute(other, "z", [(i, i ^ 1) for i in range(NZ)])
    pair = jnp.where(e == 0, jnp.stack([mine, other]), jnp.stack([other, mine]))
    strip = jnp.zeros((2, 4, 32, 512), f32)
    for d in range(NY):
        got = pair if d == 0 else lax.ppermute(pair, "col", shift_perm(NY, d))
        strip = lax.dynamic_update_slice(
            strip, got[:, None], (0, lax.rem(y + NY - d, NY), 0, 0)
        )
    strip = strip.reshape(256, 512)

    blocks = root_inverse.reshape(B, 8, B)

    def listed(target):
        out = []
        for h in range(2):
            k = lax.dynamic_index_in_dim(pattern, 2 * target + h, 0, False) - 8 * y
            ok = (k >= 0) & (k < 8)
            col = lax.dynamic_slice_in_dim(blocks, jnp.clip(k, 0, 7), 1, axis=1)
            out.append(jnp.where(ok, col.reshape(B, B), 0.0))
        return jnp.stack(out)

    cols = listed(y)
    for d in (1, 2, 3):
        sent = listed(lax.rem(y + d, NY))
        pairs = [
            (a * NY + c, a * NY + (c + d) % NY) for a in range(4) for c in range(2)
        ]
        cols = cols + lax.ppermute(sent, ("z", "col"), pairs)

    cut = cols.reshape(2, NX, 4, 8, B).transpose(0, 2, 1, 3, 4).reshape(32 * 8, B)
    cut = lax.all_to_all(cut, ("z", "x"), 0, 0, tiled=True).reshape(32, 8, B)
    kept = jnp.concatenate(
        [lax.dynamic_slice_in_dim(cut, pattern[j], 1, axis=0) for j in range(8)]
    )
    wide = jnp.broadcast_to(kept[None], (NZ, 8, 8, B)).reshape(NZ * 64, B)
    wide = lax.all_to_all(wide, "z", 0, 0, tiled=True)
    picked = (
        wide.reshape(2, 4, 8, 8, B).transpose(2, 1, 3, 0, 4).reshape(256, 256)
    )
    rows = lax.dynamic_slice_in_dim(picked, z * 32, 32, axis=0)

    share = lax.dot_general(
        picked, strip, (((0,), (0,)), ((), ())), precision=HIGH,
        preferred_element_type=f32,
    ).reshape(256, NX, B)

    def share_of(t):
        return lax.dynamic_slice_in_dim(share, t, 1, axis=1).reshape(256, B)

    total = share_of(x)
    for d in (1, 2, 3):
        total = total + lax.ppermute(
            share_of(lax.rem(x + d, NX)), "x", shift_perm(NX, d)
        )

    both = jnp.concatenate([total, rows.reshape(32, 2, B).transpose(1, 0, 2).reshape(64, B)])
    full = jnp.zeros((NY, 320, B), f32)
    for d in range(NY):
        got = both if d == 0 else lax.ppermute(both, "col", shift_perm(NY, d))
        full = lax.dynamic_update_slice(full, got[None], (lax.rem(y + NY - d, NY), 0, 0))
    product = full[:, :256].reshape(1024, B)
    picked_rows = full[:, 256:].reshape(NY * 2, 32, B).transpose(1, 0, 2).reshape(32, 1024)

    coupling = -jnp.dot(
        picked_rows, gathered, precision=HIGH, preferred_element_type=f32
    )
    correction = lax.dot_general(
        product, gathered, (((0,), (0,)), ((), ())), precision=HIGH,
        preferred_element_type=f32,
    )
    return coupling, child_inverse + correction


def solution(mesh):
    inner = Mesh(mesh.devices.reshape(2, NZ, NX, NY), ("shift", "z", "x", "col"))
    whole = P(("shift", "z", "x"), "col")
    return jax.shard_map(
        shards,
        mesh=inner,
        in_specs=(whole, P("shift"), whole, whole),
        out_specs=(whole, whole),
        check_vma=False,
    )
```

```python
import jax
import jax.numpy as jnp
from jax import lax
from jax.experimental import pallas as pl
from jax.experimental.pallas import tpu as pltpu
from jax.sharding import Mesh, PartitionSpec as P

B = 128
NZ, NX, NY = 8, 4, 4
HIGH = lax.Precision.HIGH


def shift_perm(n, d):
    return [(i, (i + d) % n) for i in range(n)]


def zxy(z, x, y):
    return (z * NX + x) * NY + y


def list_kernel(pattern_ref, y_ref, root_ref, out_ref):
    for m in range(8):
        k = pattern_ref[m] - 8 * y_ref[0]
        ok = jnp.logical_and(k >= 0, k < 8)
        start = pl.multiple_of(jnp.clip(k, 0, 7) * B, B)
        out_ref[m] = jnp.where(ok, root_ref[:, pl.ds(start, B)], 0.0)


def keep_kernel(pattern_ref, cut_ref, out_ref):
    rows = [cut_ref[pattern_ref[j]] for j in range(8)]
    for t in range(NZ):
        for j in range(8):
            out_ref[t, j] = rows[j]


def scalar_spec():
    return pl.BlockSpec(memory_space=pltpu.SMEM)


def vmem_spec():
    return pl.BlockSpec(memory_space=pltpu.VMEM)


def shards(root_inverse, pattern, child_rows, child_inverse):
    z = lax.axis_index("z")
    x = lax.axis_index("x")
    y = lax.axis_index("col")
    f32 = jnp.float32

    listed = pl.pallas_call(
        list_kernel,
        out_shape=jax.ShapeDtypeStruct((8, B, B), f32),
        in_specs=[scalar_spec(), scalar_spec(), vmem_spec()],
        out_specs=vmem_spec(),
    )(pattern, y.astype(jnp.int32).reshape(1), root_inverse)

    def listed_for(target):
        return lax.dynamic_slice_in_dim(listed, 2 * target, 2, axis=0)

    cols = listed_for(y)
    for d in (1, 2, 3):
        pairs = [
            (a * NY + c, a * NY + (c + d) % NY) for a in range(4) for c in range(2)
        ]
        cols = cols + lax.ppermute(
            listed_for(lax.rem(y + d, NY)), ("z", "col"), pairs
        )

    parts = [child_rows] + [
        lax.ppermute(child_rows, "x", shift_perm(NX, d)) for d in (1, 2, 3)
    ]
    block = jnp.zeros((NX, 32, 1024), f32)
    for d in range(NX):
        block = lax.dynamic_update_slice(
            block, parts[d][None], (lax.rem(x + NX - d, NX), 0, 0)
        )
    block = block.reshape(B, 1024)

    e = lax.rem(z, 2)
    high = z // 4
    halves = child_rows.reshape(32, 2, 512)
    places = [(a, b, c) for a in range(NZ) for b in range(NX) for c in range(NY)]
    straight = [
        (zxy(a, b, c), zxy(2 * c + a // 4, b, a % 4)) for a, b, c in places
    ]
    crossed = [
        (zxy(a, b, c), zxy(2 * c + 1 - a // 4, b, a % 4)) for a, b, c in places
    ]
    mine = lax.ppermute(
        lax.dynamic_slice_in_dim(halves, high, 1, axis=1).reshape(32, 512),
        ("z", "x", "col"), straight,
    )
    other = lax.ppermute(
        lax.dynamic_slice_in_dim(halves, 1 - high, 1, axis=1).reshape(32, 512),
        ("z", "x", "col"), crossed,
    )
    pair = jnp.where(e == 0, jnp.stack([mine, other]), jnp.stack([other, mine]))
    strip = jnp.zeros((2, 4, 32, 512), f32)
    for d in range(NY):
        got = pair if d == 0 else lax.ppermute(pair, "col", shift_perm(NY, d))
        strip = lax.dynamic_update_slice(
            strip, got[:, None], (0, lax.rem(y + NY - d, NY), 0, 0)
        )
    strip = strip.reshape(256, 512)

    gathered = jnp.zeros((NZ, B, 1024), f32)

    def place(whole, part, d, column=0):
        return lax.dynamic_update_slice(
            whole, part[None], (lax.rem(z + 2 * NZ - d, NZ), 0, column)
        )

    gathered = place(gathered, block, 0)
    up = down = block
    for step in (1, 2, 3):
        up = lax.ppermute(up, "z", shift_perm(NZ, 1))
        down = lax.ppermute(down, "z", shift_perm(NZ, -1))
        gathered = place(gathered, up, step)
        gathered = place(gathered, down, -step)
    left = lax.ppermute(up[:, :512], "z", shift_perm(NZ, 1))
    right = lax.ppermute(down[:, 512:], "z", shift_perm(NZ, -1))
    gathered = place(gathered, left, 4)
    gathered = place(gathered, right, 4, 512)
    gathered = gathered.reshape(1024, 1024)

    cut = cols.reshape(2, NX, 4, 8, B).transpose(0, 2, 1, 3, 4).reshape(32 * 8, B)
    cut = lax.all_to_all(cut, ("z", "x"), 0, 0, tiled=True).reshape(32, 8, B)
    wide = pl.pallas_call(
        keep_kernel,
        out_shape=jax.ShapeDtypeStruct((NZ, 8, 8, B), f32),
        in_specs=[scalar_spec(), vmem_spec()],
        out_specs=vmem_spec(),
    )(pattern, cut).reshape(NZ * 64, B)
    wide = lax.all_to_all(wide, "z", 0, 0, tiled=True)
    picked = (
        wide.reshape(2, 4, 8, 8, B).transpose(2, 1, 3, 0, 4).reshape(256, 256)
    )
    rows = lax.dynamic_slice_in_dim(picked, z * 32, 32, axis=0)

    share = lax.dot_general(
        picked, strip, (((0,), (0,)), ((), ())), precision=HIGH,
        preferred_element_type=f32,
    ).reshape(256, NX, B)

    def share_of(t):
        return lax.dynamic_slice_in_dim(share, t, 1, axis=1).reshape(256, B)

    total = share_of(x)
    for d in (1, 2, 3):
        total = total + lax.ppermute(
            share_of(lax.rem(x + d, NX)), "x", shift_perm(NX, d)
        )

    both = jnp.concatenate(
        [total, rows.reshape(32, 2, B).transpose(1, 0, 2).reshape(64, B)]
    )
    full = jnp.zeros((NY, 320, B), f32)
    for d in range(NY):
        got = both if d == 0 else lax.ppermute(both, "col", shift_perm(NY, d))
        full = lax.dynamic_update_slice(full, got[None], (lax.rem(y + NY - d, NY), 0, 0))
    product = full[:, :256].reshape(1024, B)
    picked_rows = full[:, 256:].reshape(8, 32, B).transpose(0, 2, 1).reshape(1024, 32)

    last = lax.dot_general(
        jnp.concatenate([product, -picked_rows], axis=1), gathered,
        (((0,), (0,)), ((), ())), precision=HIGH, preferred_element_type=f32,
    )
    return last[B:], child_inverse + last[:B]


def solution(mesh):
    inner = Mesh(mesh.devices.reshape(2, NZ, NX, NY), ("shift", "z", "x", "col"))
    whole = P(("shift", "z", "x"), "col")
    return jax.shard_map(
        shards,
        mesh=inner,
        in_specs=(whole, P("shift"), whole, whole),
        out_specs=(whole, whole),
        check_vma=False,
    )
```

```python
import jax
import jax.numpy as jnp
from jax import lax
from jax.experimental import pallas as pl
from jax.experimental.pallas import tpu as pltpu
from jax.sharding import Mesh, PartitionSpec as P

B = 128
NZ, NX, NY = 8, 4, 4
HIGH = lax.Precision.HIGH


def shift_perm(n, d):
    return [(i, (i + d) % n) for i in range(n)]


def after(value, *done):
    return lax.optimization_barrier((value, *done))[0]


def zxy(z, x, y):
    return (z * NX + x) * NY + y


def list_kernel(pattern_ref, y_ref, root_ref, out_ref):
    for m in range(8):
        k = jnp.clip(pattern_ref[m] - 8 * y_ref[0], 0, 7)
        column = root_ref[:, pl.ds(pl.multiple_of(k * B, B), B)]
        for row in range(16):
            out_ref[m % 2, row % 4, row // 4, m // 2] = column[8 * row : 8 * row + 8]


def keep_kernel(pattern_ref, m_ref, cut_ref, out_ref):
    owner = pattern_ref[m_ref[0]] // 8
    rows = [cut_ref[pattern_ref[j] * NY + owner] for j in range(8)]
    for t in range(NZ):
        for j in range(8):
            out_ref[t, j] = rows[j]


def scalar_spec():
    return pl.BlockSpec(memory_space=pltpu.SMEM)


def vmem_spec():
    return pl.BlockSpec(memory_space=pltpu.VMEM)


def shards(root_inverse, pattern, child_rows, child_inverse):
    z = lax.axis_index("z")
    x = lax.axis_index("x")
    y = lax.axis_index("col")
    f32 = jnp.float32

    parts = [child_rows] + [
        lax.ppermute(child_rows, "x", shift_perm(NX, d)) for d in (1, 2, 3)
    ]
    block = jnp.zeros((NX, 32, 1024), f32)
    for d in range(NX):
        block = lax.dynamic_update_slice(
            block, parts[d][None], (lax.rem(x + NX - d, NX), 0, 0)
        )
    block = block.reshape(B, 1024)

    e = lax.rem(z, 2)
    high = z // 4
    halves = after(child_rows, block).reshape(32, 2, 512)
    places = [(a, b, c) for a in range(NZ) for b in range(NX) for c in range(NY)]
    straight = [
        (zxy(a, b, c), zxy(2 * c + a // 4, b, a % 4)) for a, b, c in places
    ]
    crossed = [
        (zxy(a, b, c), zxy(2 * c + 1 - a // 4, b, a % 4)) for a, b, c in places
    ]
    mine = lax.ppermute(
        lax.dynamic_slice_in_dim(halves, high, 1, axis=1).reshape(32, 512),
        ("z", "x", "col"), straight,
    )
    other = lax.ppermute(
        lax.dynamic_slice_in_dim(halves, 1 - high, 1, axis=1).reshape(32, 512),
        ("z", "x", "col"), crossed,
    )
    pair = jnp.where(e == 0, jnp.stack([mine, other]), jnp.stack([other, mine]))
    strip = jnp.zeros((2, 4, 32, 512), f32)
    for d in range(NY):
        got = pair if d == 0 else lax.ppermute(pair, "col", shift_perm(NY, d))
        strip = lax.dynamic_update_slice(
            strip, got[:, None], (0, lax.rem(y + NY - d, NY), 0, 0)
        )
    strip = strip.reshape(256, 512)

    gathered = jnp.zeros((NZ, B, 1024), f32)

    def place(whole, part, d, column=0):
        return lax.dynamic_update_slice(
            whole, part[None], (lax.rem(z + 2 * NZ - d, NZ), 0, column)
        )

    gathered = place(gathered, block, 0)
    up = down = block
    ring = []
    for step in (1, 2, 3):
        up = lax.ppermute(up, "z", shift_perm(NZ, 1))
        down = lax.ppermute(down, "z", shift_perm(NZ, -1))
        ring.append((up, down))
        gathered = place(gathered, up, step)
        gathered = place(gathered, down, -step)
    left = lax.ppermute(up[:, :512], "z", shift_perm(NZ, 1))
    right = lax.ppermute(down[:, 512:], "z", shift_perm(NZ, -1))
    gathered = place(gathered, left, 4)
    gathered = place(gathered, right, 4, 512)
    gathered = gathered.reshape(1024, 1024)

    listed = pl.pallas_call(
        list_kernel,
        out_shape=jax.ShapeDtypeStruct((2, 4, NX, NY, 8, B), f32),
        in_specs=[scalar_spec(), scalar_spec(), vmem_spec()],
        out_specs=vmem_spec(),
    )(pattern, y.astype(jnp.int32).reshape(1), root_inverse)
    listed = after(listed.reshape(128 * 8, B), block)
    cut = lax.all_to_all(listed, ("z", "x", "col"), 0, 0, tiled=True)
    wide = pl.pallas_call(
        keep_kernel,
        out_shape=jax.ShapeDtypeStruct((NZ, 8, 8, B), f32),
        in_specs=[scalar_spec(), scalar_spec(), vmem_spec()],
        out_specs=vmem_spec(),
    )(pattern, (2 * y + high).astype(jnp.int32).reshape(1), cut.reshape(128, 8, B))
    wide = after(wide.reshape(NZ * 64, B), *ring[0])
    wide = lax.all_to_all(wide, "z", 0, 0, tiled=True)
    picked = (
        wide.reshape(2, 4, 8, 8, B).transpose(2, 1, 3, 0, 4).reshape(256, 256)
    )
    rows = lax.dynamic_slice_in_dim(picked, z * 32, 32, axis=0)

    share = lax.dot_general(
        picked, strip, (((0,), (0,)), ((), ())), precision=HIGH,
        preferred_element_type=f32,
    ).reshape(256, NX, B)
    share = after(share, *ring[1])

    def share_of(t):
        return lax.dynamic_slice_in_dim(share, t, 1, axis=1).reshape(256, B)

    total = share_of(x)
    for d in (1, 2, 3):
        total = total + lax.ppermute(
            share_of(lax.rem(x + d, NX)), "x", shift_perm(NX, d)
        )

    both = jnp.concatenate(
        [total, rows.reshape(32, 2, B).transpose(1, 0, 2).reshape(64, B)]
    )
    full = jnp.zeros((NY, 320, B), f32)
    for d in range(NY):
        got = both if d == 0 else lax.ppermute(both, "col", shift_perm(NY, d))
        full = lax.dynamic_update_slice(full, got[None], (lax.rem(y + NY - d, NY), 0, 0))
    full = after(full, *ring[2])
    product = full[:, :256].reshape(1024, B)
    picked_rows = full[:, 256:].reshape(8, 32, B).transpose(0, 2, 1).reshape(1024, 32)

    last = lax.dot_general(
        jnp.concatenate([product, -picked_rows], axis=1), gathered,
        (((0,), (0,)), ((), ())), precision=HIGH, preferred_element_type=f32,
    )
    return last[B:], child_inverse + last[:B]


def solution(mesh):
    inner = Mesh(mesh.devices.reshape(2, NZ, NX, NY), ("shift", "z", "x", "col"))
    whole = P(("shift", "z", "x"), "col")
    return jax.shard_map(
        shards,
        mesh=inner,
        in_specs=(whole, P("shift"), whole, whole),
        out_specs=(whole, whole),
        check_vma=False,
    )
```

```python
import jax
import jax.numpy as jnp
from jax import lax
from jax.experimental import pallas as pl
from jax.experimental.pallas import tpu as pltpu
from jax.sharding import Mesh, PartitionSpec as P

B = 128
NZ, NX, NY = 8, 4, 4
HIGH = lax.Precision.HIGH


def shift_perm(n, d):
    return [(i, (i + d) % n) for i in range(n)]


def after(value, *done):
    return lax.optimization_barrier((value, *done))[0]


def zxy(z, x, y):
    return (z * NX + x) * NY + y


def list_kernel(pattern_ref, y_ref, root_ref, out_ref):
    for m in range(8):
        k = jnp.clip(pattern_ref[m] - 8 * y_ref[0], 0, 7)
        column = root_ref[:, pl.ds(pl.multiple_of(k * B, B), B)]
        for row in range(16):
            out_ref[m % 2, row % 4, row // 4, m // 2] = column[8 * row : 8 * row + 8]


def keep_kernel(pattern_ref, m_ref, cut_ref, out_ref):
    owner = pattern_ref[m_ref[0]] // 8
    rows = [cut_ref[pattern_ref[j] * NY + owner] for j in range(8)]
    for t in range(NZ):
        for j in range(8):
            out_ref[t, j] = rows[j]


def last_kernel(
    far_ref, product_ref, rows_ref, block_ref, left_ref, right_ref, inverse_ref,
    coupling_ref, out_ref, hi, lo,
):
    @pl.when(pl.program_id(0) == 0)
    def _():
        left = jnp.concatenate([product_ref[...].T, -rows_ref[...]], axis=0)
        high = left.astype(jnp.bfloat16)
        hi[...] = high
        lo[...] = (left - high.astype(jnp.float32)).astype(jnp.bfloat16)

    def dot(a, b):
        return jnp.dot(a, b, preferred_element_type=jnp.float32)

    def dot3(a_high, a_low, block):
        high = block.astype(jnp.bfloat16)
        low = (block - high.astype(jnp.float32)).astype(jnp.bfloat16)
        return dot(a_high, low) + dot(a_low, high) + dot(a_high, high)

    far = pl.ds(pl.multiple_of(far_ref[0] * B, B), B)
    half = jnp.where(pl.program_id(0) < 2, left_ref[...], right_ref[...])
    total = dot3(hi[...], lo[...], block_ref[...]) + dot3(hi[:, far], lo[:, far], half)
    out_ref[...] = inverse_ref[...] + total[:B]
    coupling_ref[...] = total[B:]


def scalar_spec():
    return pl.BlockSpec(memory_space=pltpu.SMEM)


def vmem_spec():
    return pl.BlockSpec(memory_space=pltpu.VMEM)


def shards(root_inverse, pattern, child_rows, child_inverse):
    z = lax.axis_index("z")
    x = lax.axis_index("x")
    y = lax.axis_index("col")
    f32 = jnp.float32

    parts = [child_rows] + [
        lax.ppermute(child_rows, "x", shift_perm(NX, d)) for d in (1, 2, 3)
    ]
    block = jnp.zeros((NX, 32, 1024), f32)
    for d in range(NX):
        block = lax.dynamic_update_slice(
            block, parts[d][None], (lax.rem(x + NX - d, NX), 0, 0)
        )
    block = block.reshape(B, 1024)

    e = lax.rem(z, 2)
    high = z // 4
    turned = after(child_rows, block)
    first, second = turned[:, :512], turned[:, 512:]
    places = [(a, b, c) for a in range(NZ) for b in range(NX) for c in range(NY)]
    straight = [
        (zxy(a, b, c), zxy(2 * c + a // 4, b, a % 4)) for a, b, c in places
    ]
    crossed = [
        (zxy(a, b, c), zxy(2 * c + 1 - a // 4, b, a % 4)) for a, b, c in places
    ]
    mine = lax.ppermute(
        jnp.where(high == 0, first, second),
        ("z", "x", "col"), straight,
    )
    other = lax.ppermute(
        jnp.where(high == 0, second, first),
        ("z", "x", "col"), crossed,
    )
    pair = jnp.where(e == 0, jnp.stack([mine, other]), jnp.stack([other, mine]))
    strip = jnp.zeros((2, 4, 32, 512), f32)
    for d in range(NY):
        got = pair if d == 0 else lax.ppermute(pair, "col", shift_perm(NY, d))
        strip = lax.dynamic_update_slice(
            strip, got[:, None], (0, lax.rem(y + NY - d, NY), 0, 0)
        )
    strip = strip.reshape(256, 512)

    gathered = jnp.zeros((NZ, B, 1024), f32)

    def place(whole, part, d, column=0):
        return lax.dynamic_update_slice(
            whole, part[None], (lax.rem(z + 2 * NZ - d, NZ), 0, column)
        )

    gathered = place(gathered, block, 0)
    up = down = block
    ring = []
    for step in (1, 2, 3):
        up = lax.ppermute(up, "z", shift_perm(NZ, 1))
        down = lax.ppermute(down, "z", shift_perm(NZ, -1))
        ring.append((up, down))
        gathered = place(gathered, up, step)
        gathered = place(gathered, down, -step)
    left = lax.ppermute(up[:, :512], "z", shift_perm(NZ, 1))
    right = lax.ppermute(down[:, 512:], "z", shift_perm(NZ, -1))
    gathered = gathered.reshape(1024, 1024)

    listed = pl.pallas_call(
        list_kernel,
        out_shape=jax.ShapeDtypeStruct((2, 4, NX, NY, 8, B), f32),
        in_specs=[scalar_spec(), scalar_spec(), vmem_spec()],
        out_specs=vmem_spec(),
    )(pattern, y.astype(jnp.int32).reshape(1), root_inverse)
    listed = after(listed.reshape(128 * 8, B), block)
    cut = lax.all_to_all(listed, ("z", "x", "col"), 0, 0, tiled=True)
    wide = pl.pallas_call(
        keep_kernel,
        out_shape=jax.ShapeDtypeStruct((NZ, 8, 8, B), f32),
        in_specs=[scalar_spec(), scalar_spec(), vmem_spec()],
        out_specs=vmem_spec(),
    )(pattern, (2 * y + high).astype(jnp.int32).reshape(1), cut.reshape(128, 8, B))
    wide = after(wide.reshape(NZ * 64, B), *ring[0])
    wide = lax.all_to_all(wide, "z", 0, 0, tiled=True)
    picked = (
        wide.reshape(2, 4, 8, 8, B).transpose(2, 1, 3, 0, 4).reshape(256, 256)
    )
    rows = lax.dynamic_slice_in_dim(picked, z * 32, 32, axis=0)

    share = lax.dot_general(
        picked, strip, (((0,), (0,)), ((), ())), precision=HIGH,
        preferred_element_type=f32,
    ).reshape(256, NX, B)
    share = after(share, *ring[1])

    def share_of(t):
        return lax.dynamic_slice_in_dim(share, t, 1, axis=1).reshape(256, B)

    total = share_of(x)
    for d in (1, 2, 3):
        total = total + lax.ppermute(
            share_of(lax.rem(x + d, NX)), "x", shift_perm(NX, d)
        )

    both = jnp.concatenate(
        [total, rows.reshape(32, 2, B).transpose(1, 0, 2).reshape(64, B)]
    )
    full = jnp.zeros((NY, 320, B), f32)
    for d in range(NY):
        got = both if d == 0 else lax.ppermute(both, "col", shift_perm(NY, d))
        full = lax.dynamic_update_slice(full, got[None], (lax.rem(y + NY - d, NY), 0, 0))
    full = after(full, gathered)
    product = full[:, :256].reshape(1024, B)
    picked_rows = full[:, 256:].reshape(8, 32, B).transpose(1, 0, 2).reshape(32, 1024)

    opposite = lax.rem(z + 4, NZ).astype(jnp.int32).reshape(1)

    def columns(height):
        return pl.BlockSpec((height, 256), lambda i: (0, i))

    return pl.pallas_call(
        last_kernel,
        grid=(4,),
        out_shape=[
            jax.ShapeDtypeStruct((32, 1024), f32),
            jax.ShapeDtypeStruct((B, 1024), f32),
        ],
        in_specs=[
            scalar_spec(),
            pl.BlockSpec((1024, B), lambda i: (0, 0)),
            pl.BlockSpec((32, 1024), lambda i: (0, 0)),
            columns(1024),
            pl.BlockSpec((B, 256), lambda i: (0, jnp.minimum(i, 1))),
            pl.BlockSpec((B, 256), lambda i: (0, jnp.maximum(i - 2, 0))),
            columns(B),
        ],
        out_specs=[columns(32), columns(B)],
        scratch_shapes=[pltpu.VMEM((B + 32, 1024), jnp.bfloat16)] * 2,
        compiler_params=pltpu.CompilerParams(vmem_limit_bytes=32 * 1024 * 1024),
    )(opposite, product, picked_rows, gathered, left, right, child_inverse)


def solution(mesh):
    inner = Mesh(mesh.devices.reshape(2, NZ, NX, NY), ("shift", "z", "x", "col"))
    whole = P(("shift", "z", "x"), "col")
    return jax.shard_map(
        shards,
        mesh=inner,
        in_specs=(whole, P("shift"), whole, whole),
        out_specs=(whole, whole),
        check_vma=False,
    )
```

```python
import jax
import jax.numpy as jnp
from jax import lax
from jax.experimental import pallas as pl
from jax.experimental.pallas import tpu as pltpu
from jax.sharding import Mesh, PartitionSpec as P

B = 128
NZ, NX, NY = 8, 4, 4
HIGH = lax.Precision.HIGH


def shift_perm(n, d):
    return [(i, (i + d) % n) for i in range(n)]


def after(value, *done):
    return lax.optimization_barrier((value, *done))[0]


def zxy(z, x, y):
    return (z * NX + x) * NY + y


def list_kernel(pattern_ref, y_ref, root_ref, out_ref):
    for m in range(8):
        k = jnp.clip(pattern_ref[m] - 8 * y_ref[0], 0, 7)
        column = root_ref[:, pl.ds(pl.multiple_of(k * B, B), B)]
        for row in range(16):
            out_ref[m % 2, row % 4, row // 4, m // 2] = column[8 * row : 8 * row + 8]


def keep_kernel(pattern_ref, m_ref, cut_ref, out_ref):
    owner = pattern_ref[m_ref[0]] // 8
    rows = [cut_ref[pattern_ref[j] * NY + owner] for j in range(8)]
    for t in range(NZ):
        for j in range(8):
            out_ref[t, j] = rows[j]


def last_kernel(
    far_ref, product_ref, rows_ref, block_ref, left_ref, right_ref, inverse_ref,
    coupling_ref, out_ref, halves,
):
    @pl.when(pl.program_id(0) == 0)
    def _():
        left = jnp.concatenate([product_ref[...].T, -rows_ref[...]], axis=0)
        high = left.astype(jnp.bfloat16)
        halves[: B + 32] = high
        halves[B + 32 :] = (left - high.astype(jnp.float32)).astype(jnp.bfloat16)

    def dot(a, b):
        return jnp.dot(a, b, preferred_element_type=jnp.float32)

    def dot3(a, block):
        high = block.astype(jnp.bfloat16)
        low = (block - high.astype(jnp.float32)).astype(jnp.bfloat16)
        both = dot(a, high)
        return dot(a[: B + 32], low) + both[B + 32 :] + both[: B + 32]

    far = pl.ds(pl.multiple_of(far_ref[0] * B, B), B)
    half = jnp.where(pl.program_id(0) < 2, left_ref[...], right_ref[...])
    total = dot3(halves[...], block_ref[...]) + dot3(halves[:, far], half)
    out_ref[...] = inverse_ref[...] + total[:B]
    coupling_ref[...] = total[B:]


def scalar_spec():
    return pl.BlockSpec(memory_space=pltpu.SMEM)


def vmem_spec():
    return pl.BlockSpec(memory_space=pltpu.VMEM)


def shards(root_inverse, pattern, child_rows, child_inverse):
    z = lax.axis_index("z")
    x = lax.axis_index("x")
    y = lax.axis_index("col")
    f32 = jnp.float32

    parts = [child_rows] + [
        lax.ppermute(child_rows, "x", shift_perm(NX, d)) for d in (1, 2, 3)
    ]
    block = jnp.zeros((NX, 32, 1024), f32)
    for d in range(NX):
        block = lax.dynamic_update_slice(
            block, parts[d][None], (lax.rem(x + NX - d, NX), 0, 0)
        )
    block = block.reshape(B, 1024)

    e = lax.rem(z, 2)
    high = z // 4
    turned = after(child_rows, block)
    first, second = turned[:, :512], turned[:, 512:]
    places = [(a, b, c) for a in range(NZ) for b in range(NX) for c in range(NY)]
    straight = [
        (zxy(a, b, c), zxy(2 * c + a // 4, b, a % 4)) for a, b, c in places
    ]
    crossed = [
        (zxy(a, b, c), zxy(2 * c + 1 - a // 4, b, a % 4)) for a, b, c in places
    ]
    mine = lax.ppermute(
        jnp.where(high == 0, first, second),
        ("z", "x", "col"), straight,
    )
    other = lax.ppermute(
        jnp.where(high == 0, second, first),
        ("z", "x", "col"), crossed,
    )
    pair = jnp.where(e == 0, jnp.stack([mine, other]), jnp.stack([other, mine]))
    strip = jnp.zeros((2, 4, 32, 512), f32)
    for d in range(NY):
        got = pair if d == 0 else lax.ppermute(pair, "col", shift_perm(NY, d))
        strip = lax.dynamic_update_slice(
            strip, got[:, None], (0, lax.rem(y + NY - d, NY), 0, 0)
        )
    strip = strip.reshape(256, 512)

    gathered = jnp.zeros((NZ, B, 1024), f32)

    def place(whole, part, d, column=0):
        return lax.dynamic_update_slice(
            whole, part[None], (lax.rem(z + 2 * NZ - d, NZ), 0, column)
        )

    gathered = place(gathered, block, 0)
    up = down = block
    ring = []
    for step in (1, 2, 3):
        up = lax.ppermute(up, "z", shift_perm(NZ, 1))
        down = lax.ppermute(down, "z", shift_perm(NZ, -1))
        ring.append((up, down))
        gathered = place(gathered, up, step)
        gathered = place(gathered, down, -step)
    left = lax.ppermute(up[:, :512], "z", shift_perm(NZ, 1))
    right = lax.ppermute(down[:, 512:], "z", shift_perm(NZ, -1))
    gathered = gathered.reshape(1024, 1024)

    listed = pl.pallas_call(
        list_kernel,
        out_shape=jax.ShapeDtypeStruct((2, 4, NX, NY, 8, B), f32),
        in_specs=[scalar_spec(), scalar_spec(), vmem_spec()],
        out_specs=vmem_spec(),
    )(pattern, y.astype(jnp.int32).reshape(1), root_inverse)
    listed = after(listed.reshape(128 * 8, B), block)
    cut = lax.all_to_all(listed, ("z", "x", "col"), 0, 0, tiled=True)
    wide = pl.pallas_call(
        keep_kernel,
        out_shape=jax.ShapeDtypeStruct((NZ, 8, 8, B), f32),
        in_specs=[scalar_spec(), scalar_spec(), vmem_spec()],
        out_specs=vmem_spec(),
    )(pattern, (2 * y + high).astype(jnp.int32).reshape(1), cut.reshape(128, 8, B))
    wide = after(wide.reshape(NZ * 64, B), *ring[0])
    wide = lax.all_to_all(wide, "z", 0, 0, tiled=True)
    picked = (
        wide.reshape(2, 4, 8, 8, B).transpose(2, 1, 3, 0, 4).reshape(256, 256)
    )
    rows = lax.dynamic_slice_in_dim(picked, z * 32, 32, axis=0)

    share = lax.dot_general(
        picked, strip, (((0,), (0,)), ((), ())), precision=HIGH,
        preferred_element_type=f32,
    ).reshape(256, NX, B)
    share = after(share, *ring[1])

    def share_of(t):
        return lax.dynamic_slice_in_dim(share, t, 1, axis=1).reshape(256, B)

    total = share_of(x)
    for d in (1, 2, 3):
        total = total + lax.ppermute(
            share_of(lax.rem(x + d, NX)), "x", shift_perm(NX, d)
        )

    both = jnp.concatenate(
        [total, rows.reshape(32, 2, B).transpose(1, 0, 2).reshape(64, B)]
    )
    full = jnp.zeros((NY, 320, B), f32)
    for d in range(NY):
        got = both if d == 0 else lax.ppermute(both, "col", shift_perm(NY, d))
        full = lax.dynamic_update_slice(full, got[None], (lax.rem(y + NY - d, NY), 0, 0))
    full = after(full, gathered)
    product = full[:, :256].reshape(1024, B)
    picked_rows = full[:, 256:].reshape(8, 32, B).transpose(1, 0, 2).reshape(32, 1024)

    opposite = lax.rem(z + 4, NZ).astype(jnp.int32).reshape(1)

    def columns(height):
        return pl.BlockSpec((height, 256), lambda i: (0, i))

    return pl.pallas_call(
        last_kernel,
        grid=(4,),
        out_shape=[
            jax.ShapeDtypeStruct((32, 1024), f32),
            jax.ShapeDtypeStruct((B, 1024), f32),
        ],
        in_specs=[
            scalar_spec(),
            pl.BlockSpec((1024, B), lambda i: (0, 0)),
            pl.BlockSpec((32, 1024), lambda i: (0, 0)),
            columns(1024),
            pl.BlockSpec((B, 256), lambda i: (0, jnp.minimum(i, 1))),
            pl.BlockSpec((B, 256), lambda i: (0, jnp.maximum(i - 2, 0))),
            columns(B),
        ],
        out_specs=[columns(32), columns(B)],
        scratch_shapes=[pltpu.VMEM((2 * (B + 32), 1024), jnp.bfloat16)],
        compiler_params=pltpu.CompilerParams(vmem_limit_bytes=32 * 1024 * 1024),
    )(opposite, product, picked_rows, gathered, left, right, child_inverse)


def solution(mesh):
    inner = Mesh(mesh.devices.reshape(2, NZ, NX, NY), ("shift", "z", "x", "col"))
    whole = P(("shift", "z", "x"), "col")
    return jax.shard_map(
        shards,
        mesh=inner,
        in_specs=(whole, P("shift"), whole, whole),
        out_specs=(whole, whole),
        check_vma=False,
    )
```
